256 devices in a mesh: grp: 128 (over x, y_hi, z, core), wide: 2 (over y_lo).
Axes of the slice: x: 4, y: 4 (y_hi: 2, y_lo: 2; y = y_hi * 2 + y_lo), z: 8, core: 2. Of those that a mesh axis runs over, the one named last changes fastest.
Arguments:
- ao_slab: bfloat16 [1024, 1200, 1200], P(('grp', 'wide')), may hold values from -6 to 6
- screen_mask: int32 [1024, 25, 25], P(('grp', 'wide')), may hold values 0 or 1
- pair_ao: int32 [1024, 2], P(('grp', 'wide')), may hold values from 0 to 1199
- occ_coef: bfloat16 [1200, 256], replicated, may hold values from -0.1875 to 0.1875
- vir_coef: bfloat16 [1200, 900], replicated, may hold values from -0.1875 to 0.1875
Outputs:
- mo_block: bfloat16 [256, 900, 1, 900], P(('grp', 'wide'))
The draws below stay inside these ranges and needn't reach their ends.
All inputs are finite; a program needn't handle non-finite values. No bound on the sum of `screen_mask` on one device may be relied on, other than what follows from the above.
Results may differ from the reference program's by a relative error of at most 0.007.
Values may be sent and summed in bfloat16 or wider, within the bound.
A program may use at most 128 MiB of HBM per device.

```python
import jax
import jax.numpy as jnp
from jax import lax

NBF = 1200
NOCC = 256
NVIR = 900
JWIN = 1
PAIRS = 1024
NBLK = 25


def with_ends(entries, key, low, top_value):
    shape = entries.shape
    index_at = [jax.random.randint(jax.random.fold_in(key, axis), (), 0, shape[axis]) for axis in range(len(shape))]
    entries = entries.at[tuple(index_at)].set(low)
    longest = shape.index(max(shape))
    index_at[longest] = (index_at[longest] + 1) % shape[longest]
    return entries.at[tuple(index_at)].set(top_value)


def levels(key, extent, cuts, low, high):
    def one(axis_at, shards_of):
        steps = jax.random.uniform(jax.random.fold_in(jax.random.fold_in(key, 6), axis_at), (shards_of,), jnp.float32, low / len(cuts), high / len(cuts))
        return jnp.repeat(jnp.exp(steps), extent[axis_at] // shards_of).reshape((-1,) + (1,) * (len(extent) - axis_at - 1))

    gain = one(*cuts[0])
    for cut in cuts[1:]:
        gain = gain * one(*cut)
    return gain


def gaussian(key, extent, width, reach, split=(), kind=jnp.bfloat16):
    values = width * jax.random.normal(key, extent, jnp.float32)
    if split:
        values = values * levels(key, extent, split, -0.22, 0.18)
    return jnp.clip(values, -reach, reach).astype(kind)


def setup_inputs(seed: int = 0) -> dict:
    key_of = jax.random.split(jax.random.key(seed), 6)
    return {
        "ao_slab": gaussian(key_of[0], (PAIRS, NBF, NBF), 1.0, 6.0, ((0, 256),)),
        "screen_mask": with_ends((jax.random.randint(key_of[1], (PAIRS, NBLK, NBLK), 0, 4) < 3).astype(jnp.int32), jax.random.fold_in(key_of[1], 1), 0, 1),
        "pair_ao": with_ends(jax.random.randint(key_of[2], (PAIRS, 2), 0, NBF), jax.random.fold_in(key_of[2], 1), 0, NBF - 1).astype(jnp.int32),
        "occ_coef": gaussian(key_of[3], (NBF, NOCC), NBF ** -0.5, 0.1875),
        "vir_coef": gaussian(key_of[4], (NBF, NVIR), NBF ** -0.5, 0.1875),
    }


def reference(ao_slab, screen_mask, pair_ao, occ_coef, vir_coef):
    occ_full = occ_coef.astype(jnp.float32)
    vir_full = vir_coef.astype(jnp.float32)
    block_size = NBF // NBLK

    def half_transform(operands):
        integrals, keep_mask = operands
        screened = (integrals.reshape(NBLK, block_size, NBLK, block_size)
                    * keep_mask[:, None, :, None].astype(jnp.bfloat16)).reshape(NBF, NBF)
        left = jnp.dot(occ_full.T, screened.astype(jnp.float32),
                       precision=lax.Precision.HIGHEST).astype(jnp.bfloat16)
        return jnp.dot(left.astype(jnp.float32), vir_full,
                       precision=lax.Precision.HIGHEST).astype(jnp.bfloat16)

    halves = lax.map(half_transform, (ao_slab, screen_mask))
    lambda_rows = occ_full[pair_ao[:, 0].astype(jnp.int32), :JWIN]
    sigma_rows = vir_full[pair_ao[:, 1].astype(jnp.int32)]
    pair_kernel = (lambda_rows[:, :, None] * sigma_rows[:, None, :]).astype(jnp.bfloat16)
    pair_kernel = pair_kernel.reshape(PAIRS, JWIN * NVIR).astype(jnp.float32)
    flat = halves.reshape(PAIRS, NOCC * NVIR).astype(jnp.float32)
    summed = jnp.dot(flat.T, pair_kernel, precision=lax.Precision.HIGHEST)
    scaled = summed * (NBF / (PAIRS ** 0.5))
    return scaled.astype(jnp.bfloat16).reshape(NOCC, NVIR, JWIN, NVIR)
```

```python
import jax
import jax.numpy as jnp
from jax import lax
from jax.experimental import pallas as pl
from jax.experimental.pallas import tpu as pltpu
from jax.sharding import PartitionSpec as P

MESH = pl.DeviceIdType.MESH
BF16 = jnp.bfloat16
F32 = jnp.float32

NBF = 1200
NBP = 1280
NOCC = 256
NVIR = 900
NVP = 1024
NBLK = 25
BLK = NBF // NBLK
PAIRS_HERE = 4
SIDE = 16
PAIRS = 1024
SCALE = NBF / PAIRS**0.5
NN = (((1,), (0,)), ((), ()))
NT = (((1,), (1,)), ((), ()))
TN = (((0,), (0,)), ((), ()))


def dot(a, b, dims):
    return lax.dot_general(a, b, dims, preferred_element_type=F32)


def iota(shape, axis):
    return lax.broadcasted_iota(jnp.int32, shape, axis)


def one_hot(hit):
    return jnp.where(hit, 1.0, 0.0).astype(BF16)


def kernel(
    ao, mask_ref, pair_ref, occ, vir, out,
    aob, occb, virb, virt, occt, perm, mx, scr, left, half, recv, turned, final, pk, acc, outb,
    idx_own, idx_z, idx_zrow, idx_all,
    ao_sem, in_sem, out_sem, send1, recv1, send2, recv2, idx_send, idx_recv,
):
    grp = lax.axis_index("grp")
    wide = lax.axis_index("wide")
    zc = lax.rem(grp, SIDE)
    xy = lax.div(grp, SIDE) * 2 + wide

    def at(xy_of, zc_of):
        return (lax.div(xy_of, 2) * SIDE + zc_of, lax.rem(xy_of, 2))

    occ_copy = pltpu.make_async_copy(occ, occb.at[0:NBF], in_sem.at[0])
    vir_copy = pltpu.make_async_copy(vir, virb, in_sem.at[1])
    ao_copies = [pltpu.make_async_copy(ao.at[p], aob.at[p], ao_sem.at[p]) for p in range(PAIRS_HERE)]
    occ_copy.start()
    ao_copies[0].start()
    vir_copy.start()
    for p in range(1, PAIRS_HERE):
        ao_copies[p].start()

    barrier = pltpu.get_barrier_semaphore()

    def greet(k, carry):
        pl.semaphore_signal(
            barrier, inc=1, device_id=at(xy, lax.rem(zc + k, SIDE)), device_id_type=MESH
        )
        pl.semaphore_signal(
            barrier, inc=1, device_id=at(lax.rem(xy + k, SIDE), zc), device_id_type=MESH
        )
        return carry

    lax.fori_loop(1, SIDE, greet, 0)

    row = iota((NOCC, NOCC), 0)
    col = iota((NOCC, NOCC), 1)
    hi = lax.shift_right_logical(row, 4)
    lo = row & 15

    def owner(xy_of, zc_of):
        return (lax.shift_right_logical(xy_of, 1) * SIDE + zc_of) * 2 + (xy_of & 1)

    perm[0] = one_hot(col == owner(lo, hi))
    perm[1] = one_hot(col == owner(hi, lo))
    perm[2] = one_hot(col == row)
    perm[3] = one_hot(col == lo * SIDE + hi)

    block_of = iota((NBLK, NBP), 0) * BLK
    lane = iota((NBLK, NBP), 1)
    spread = one_hot((lane >= block_of) & (lane < block_of + BLK))
    for p in range(PAIRS_HERE):
        mx[p, 0:NBLK] = dot(mask_ref[:, p, :].astype(F32).astype(BF16), spread, NN)

    lane8 = iota((8, 128), 1)
    own = jnp.zeros((8, 128), jnp.int32)
    for p in range(PAIRS_HERE):
        for q in range(2):
            own = jnp.where(lane8 == 2 * p + q, pair_ref[q : q + 1, p : p + 1], own)
    idx_own[...] = own
    idx_z[zc] = own

    scr[NBF:NBP, :] = jnp.zeros((NBP - NBF, NBP), BF16)
    scr[0:NBF, NBP - 128 : NBP] = jnp.zeros((NBF, 128), BF16)
    occb[NBF:NBP, :] = jnp.zeros((NBP - NBF, NOCC), BF16)
    virt[:, NBP - 128 : NBP] = jnp.zeros((NVP, 128), BF16)
    virt[NVIR - 4 : NVP, :] = jnp.zeros((NVP - NVIR + 4, NBP), BF16)

    occ_copy.wait()
    for q in range(2):
        occt[q] = dot(perm[q], occb[...], NT).astype(BF16)

    def phase1(p, carry):
        q = lax.rem(p, 2)
        pltpu.make_async_copy(ao.at[0], aob.at[p], ao_sem.at[p]).wait()

        def screen(r, c):
            rows = pl.ds(pl.multiple_of(r * BLK, BLK), BLK)
            keep = mx[p, pl.ds(r, 1), 0:NBF].astype(BF16)
            scr[rows, 0:NBF] = aob[p, rows, :] * keep
            return c

        lax.fori_loop(0, NBLK, screen, 0)
        left[...] = dot(occt[q], scr[...], NN).astype(BF16)

        @pl.when(p == 0)
        def _():
            vir_copy.wait()
            virt[0:NVIR, 0:NBF] = virb[...]

        half[p] = dot(left[...], virt[...], NT).astype(BF16)

        @pl.when(p == 0)
        def _():
            pl.semaphore_wait(barrier, 2 * (SIDE - 1))

            def share(k, c):
                pltpu.make_async_remote_copy(
                    src_ref=idx_own, dst_ref=idx_z.at[zc],
                    send_sem=idx_send.at[0], recv_sem=idx_recv.at[0],
                    device_id=at(xy, lax.rem(zc + k, SIDE)), device_id_type=MESH,
                ).start()
                return c

            lax.fori_loop(1, SIDE, share, 0)

        me = zc + q * (xy - zc)

        def send(k, c):
            to = lax.rem(me + k, SIDE)
            pltpu.make_async_remote_copy(
                src_ref=half.at[p, pl.ds(pl.multiple_of(to * SIDE, SIDE), SIDE)],
                dst_ref=recv.at[p, pl.ds(pl.multiple_of(me * SIDE, SIDE), SIDE)],
                send_sem=send1.at[p], recv_sem=recv1.at[p],
                device_id=at(xy + q * (to - xy), to + q * (zc - to)), device_id_type=MESH,
            ).start()
            return c

        lax.fori_loop(1, SIDE, send, 0)
        mine = pl.ds(pl.multiple_of(me * SIDE, SIDE), SIDE)
        recv[p, mine] = half[p, mine]
        return carry

    lax.fori_loop(0, PAIRS_HERE, phase1, 0)

    def got(ref, sem):
        pltpu.make_async_copy(ref, ref, sem).wait()

    got(idx_z.at[0 : SIDE - 1], idx_recv.at[0])
    idx_zrow[...] = idx_z[:, 0, :]
    idx_all[xy] = idx_z[:, 0, :]

    def share2(k, c):
        pltpu.make_async_remote_copy(
            src_ref=idx_zrow, dst_ref=idx_all.at[xy],
            send_sem=idx_send.at[1], recv_sem=idx_recv.at[1],
            device_id=at(lax.rem(xy + k, SIDE), zc), device_id_type=MESH,
        ).start()
        return c

    lax.fori_loop(1, SIDE, share2, 0)
    got(idx_all.at[0 : SIDE - 1], idx_recv.at[1])

    lane_all = iota((NOCC, 128), 1)
    basis = iota((NOCC, NBP), 1)

    def build(p, c):
        table = idx_all[...].reshape(NOCC, 128).astype(F32)

        def chosen(j):
            return jnp.sum(jnp.where(lane_all == j, table, 0.0), axis=1, keepdims=True).astype(jnp.int32)

        lam = dot(one_hot(basis == chosen(2 * p)), occb[:, 0:128], NN)[:, 0:1]
        rows = dot(one_hot(basis == chosen(2 * p + 1)), virt[...], NT)
        kernel_rows = (lam * rows).astype(BF16)
        pk[p] = dot(perm[2 + lax.rem(p, 2)], kernel_rows, NN).astype(BF16)
        return c

    lax.fori_loop(0, PAIRS_HERE, build, 0)

    def phase2(p):
        q = p % 2
        got(recv.at[p, 0 : (SIDE - 1) * SIDE], recv1.at[p])
        turned[p] = dot(perm[3], recv[p], NN).astype(BF16)
        me = xy if q == 0 else zc

        def send(k, c):
            to = lax.rem(me + k, SIDE)
            pltpu.make_async_remote_copy(
                src_ref=turned.at[p, pl.ds(pl.multiple_of(to * SIDE, SIDE), SIDE)],
                dst_ref=final.at[p, pl.ds(pl.multiple_of(me * SIDE, SIDE), SIDE)],
                send_sem=send2.at[p], recv_sem=recv2.at[p],
                device_id=at(to, zc) if q == 0 else at(xy, to), device_id_type=MESH,
            ).start()
            return c

        lax.fori_loop(1, SIDE, send, 0)
        mine = pl.ds(pl.multiple_of(me * SIDE, SIDE), SIDE)
        final[p, mine] = turned[p, mine]

    def add(p, first=False, last=False):
        got(final.at[p, 0 : (SIDE - 1) * SIDE], recv2.at[p])
        for a0 in range(0, NVP, 256):
            rows = pl.ds(a0, 256)
            term = dot(final[p, :, rows], pk[p], TN)
            if not first:
                term = acc[rows] + term
            if last:
                n = min(256, NVIR - a0)
                outb[a0 : a0 + n] = (term[0:n, 0:NVIR] * SCALE).astype(BF16)
                pltpu.make_async_copy(outb.at[a0 : a0 + n], out.at[a0 : a0 + n], out_sem.at[a0 // 256]).start()
            else:
                acc[rows] = term

    phase2(0)
    phase2(1)
    phase2(2)
    add(0, first=True)
    phase2(3)
    add(2)
    add(1)
    add(3, last=True)

    for p in range(PAIRS_HERE):
        got(half.at[p, 0 : (SIDE - 1) * SIDE], send1.at[p])
        got(turned.at[p, 0 : (SIDE - 1) * SIDE], send2.at[p])
    got(idx_z.at[0 : SIDE - 1], idx_send.at[0])
    got(idx_all.at[0 : SIDE - 1], idx_send.at[1])
    for a0 in range(0, NVP, 256):
        n = min(256, NVIR - a0)
        pltpu.make_async_copy(outb.at[a0 : a0 + n], out.at[a0 : a0 + n], out_sem.at[a0 // 256]).wait()


def shards(ao_slab, screen_mask, pair_ao, occ_coef, vir_coef):
    any_space = pl.BlockSpec(memory_space=pl.ANY)
    vmem = pl.BlockSpec(memory_space=pltpu.VMEM)
    dma = pltpu.SemaphoreType.DMA
    block = pl.pallas_call(
        kernel,
        name="mo_block",
        out_shape=jax.ShapeDtypeStruct((NVIR, NVIR), BF16),
        in_specs=[any_space, vmem, vmem, any_space, any_space],
        out_specs=any_space,
        scratch_shapes=[
            pltpu.VMEM((PAIRS_HERE, NBF, NBF), BF16),
            pltpu.VMEM((NBP, NOCC), BF16),
            pltpu.VMEM((NVIR, NBF), BF16),
            pltpu.VMEM((NVP, NBP), BF16),
            pltpu.VMEM((2, NOCC, NBP), BF16),
            pltpu.VMEM((4, NOCC, NOCC), BF16),
            pltpu.VMEM((PAIRS_HERE, 32, NBP), F32),
            pltpu.VMEM((NBP, NBP), BF16),
            pltpu.VMEM((NOCC, NBP), BF16),
            pltpu.VMEM((PAIRS_HERE, NOCC, NVP), BF16),
            pltpu.VMEM((PAIRS_HERE, NOCC, NVP), BF16),
            pltpu.VMEM((PAIRS_HERE, NOCC, NVP), BF16),
            pltpu.VMEM((PAIRS_HERE, NOCC, NVP), BF16),
            pltpu.VMEM((PAIRS_HERE, NOCC, NVP), BF16),
            pltpu.VMEM((NVP, NVP), F32),
            pltpu.VMEM((NVIR, NVIR), BF16),
            pltpu.VMEM((8, 128), jnp.int32),
            pltpu.VMEM((SIDE, 8, 128), jnp.int32),
            pltpu.VMEM((SIDE, 128), jnp.int32),
            pltpu.VMEM((SIDE, SIDE, 128), jnp.int32),
            dma((PAIRS_HERE,)),
            dma((2,)),
            dma((4,)),
            dma((PAIRS_HERE,)),
            dma((PAIRS_HERE,)),
            dma((PAIRS_HERE,)),
            dma((PAIRS_HERE,)),
            dma((2,)),
            dma((2,)),
        ],
        compiler_params=pltpu.CompilerParams(
            collective_id=0, has_side_effects=True, vmem_limit_bytes=56 << 20
        ),
        cost_estimate=pl.CostEstimate(flops=7_000_000_000, bytes_accessed=16_000_000, transcendentals=0),
    )(ao_slab, screen_mask.transpose(1, 0, 2), pair_ao.T, occ_coef, vir_coef.T)
    return block.reshape(1, NVIR, 1, NVIR)


def solution(mesh):
    in_specs = (
        P(("grp", "wide"), None, None),
        P(("grp", "wide"), None, None),
        P(("grp", "wide"), None),
        P(),
        P(),
    )
    out_specs = P(("grp", "wide"), None, None, None)
    return jax.shard_map(shards, mesh=mesh, in_specs=in_specs, out_specs=out_specs, check_vma=False)
```

```python
import jax
import jax.numpy as jnp
from jax import lax
from jax.experimental import pallas as pl
from jax.experimental.pallas import tpu as pltpu
from jax.sharding import PartitionSpec as P

MESH = pl.DeviceIdType.MESH
BF16 = jnp.bfloat16
F32 = jnp.float32

NBF = 1200
NBP = 1280
NOCC = 256
NVIR = 900
NVP = 1024
WIDE = 896
REST = NVIR - WIDE
NBLK = 25
BLK = NBF // NBLK
PAIRS_HERE = 4
SIDE = 16
PAIRS = 1024
SCALE = NBF / PAIRS**0.5
NN = (((1,), (0,)), ((), ()))
NT = (((1,), (1,)), ((), ()))
TN = (((0,), (0,)), ((), ()))


def dot(a, b, dims):
    return lax.dot_general(a, b, dims, preferred_element_type=F32)


def iota(shape, axis):
    return lax.broadcasted_iota(jnp.int32, shape, axis)


def one_hot(hit):
    return jnp.where(hit, 1.0, 0.0).astype(BF16)


def kernel(
    ao, mask, pair, occ, vir, out,
    mask_ref, pair_ref, aob, occb, virb, virt, occt, perm, mx, scr, left, half, recv, turned, final,
    rest, rest_own, rest_recv, rest_turned, rest_final, pk, pkt, acc,
    idx_own, idx_z, idx_zrow, idx_all,
    ao_sem, in_sem, send1, recv1, send2, recv2, rest_send, rest_sem, idx_send, idx_recv,
):
    grp = lax.axis_index("grp")
    wide = lax.axis_index("wide")
    zc = lax.rem(grp, SIDE)
    xy = lax.div(grp, SIDE) * 2 + wide

    def at(xy_of, zc_of):
        return (lax.div(xy_of, 2) * SIDE + zc_of, lax.rem(xy_of, 2))

    occ_copy = pltpu.make_async_copy(occ, occb.at[0:NBF], in_sem.at[0])
    vir_copy = pltpu.make_async_copy(vir, virb, in_sem.at[1])
    ao_copies = [pltpu.make_async_copy(ao.at[p], aob.at[p], ao_sem.at[p]) for p in range(PAIRS_HERE)]
    mask_copy = pltpu.make_async_copy(mask, mask_ref, in_sem.at[2])
    pair_copy = pltpu.make_async_copy(pair, pair_ref, in_sem.at[3])
    mask_copy.start()
    pair_copy.start()
    occ_copy.start()
    ao_copies[0].start()
    vir_copy.start()
    for p in range(1, PAIRS_HERE):
        ao_copies[p].start()

    barrier = pltpu.get_barrier_semaphore()

    def greet(k, carry):
        pl.semaphore_signal(
            barrier, inc=1, device_id=at(xy, lax.rem(zc + k, SIDE)), device_id_type=MESH
        )
        pl.semaphore_signal(
            barrier, inc=1, device_id=at(lax.rem(xy + k, SIDE), zc), device_id_type=MESH
        )
        return carry

    lax.fori_loop(1, SIDE, greet, 0)

    row = iota((NOCC, NOCC), 0)
    col = iota((NOCC, NOCC), 1)
    hi = lax.shift_right_logical(row, 4)
    lo = row & 15

    def owner(xy_of, zc_of):
        return (lax.shift_right_logical(xy_of, 1) * SIDE + zc_of) * 2 + (xy_of & 1)

    perm[0] = one_hot(col == owner(lo, hi))
    perm[1] = one_hot(col == owner(hi, lo))
    perm[2] = one_hot(col == row)
    perm[3] = one_hot(col == lo * SIDE + hi)

    block_of = iota((NBLK, NBP), 0) * BLK
    lane = iota((NBLK, NBP), 1)
    spread = one_hot((lane >= block_of) & (lane < block_of + BLK))
    mask_copy.wait()
    for p in range(PAIRS_HERE):
        mx[p, 0:NBLK] = dot(mask_ref[:, p, :].astype(F32).astype(BF16), spread, NN)

    lane8 = iota((8, 128), 1)
    own = jnp.zeros((8, 128), jnp.int32)
    pair_copy.wait()
    for p in range(PAIRS_HERE):
        for q in range(2):
            own = jnp.where(lane8 == 2 * p + q, pair_ref[q : q + 1, p : p + 1], own)
    idx_own[...] = own
    idx_z[zc] = own

    scr[NBF:NBP, :] = jnp.zeros((NBP - NBF, NBP), BF16)
    scr[0:NBF, NBP - 128 : NBP] = jnp.zeros((NBF, 128), BF16)
    occb[NBF:NBP, :] = jnp.zeros((NBP - NBF, NOCC), BF16)
    virt[:, NBP - 128 : NBP] = jnp.zeros((NVP, 128), BF16)
    virt[NVIR - 4 : NVP, :] = jnp.zeros((NVP - NVIR + 4, NBP), BF16)

    occ_copy.wait()
    for q in range(2):
        occt[q] = dot(perm[q], occb[...], NT).astype(BF16)

    def phase1(p, carry):
        q = lax.rem(p, 2)
        pltpu.make_async_copy(ao.at[0], aob.at[p], ao_sem.at[p]).wait()

        def screen(r, c):
            rows = pl.ds(pl.multiple_of(r * BLK, BLK), BLK)
            keep = mx[p, pl.ds(r, 1), 0:NBF].astype(BF16)
            scr[rows, 0:NBF] = aob[p, rows, :] * keep
            return c

        lax.fori_loop(0, NBLK, screen, 0)
        left[...] = dot(occt[q], scr[...], NN).astype(BF16)

        @pl.when(p == 0)
        def _():
            vir_copy.wait()
            virt[0:NVIR, 0:NBF] = virb[...]

        both = dot(left[...], virt[...], NT)
        half[p] = both[:, 0:WIDE].astype(BF16)
        rest[p] = both[:, WIDE:NVP].astype(BF16)

        @pl.when(p == 0)
        def _():
            pl.semaphore_wait(barrier, 2 * (SIDE - 1))

            def share(k, c):
                pltpu.make_async_remote_copy(
                    src_ref=idx_own, dst_ref=idx_z.at[zc],
                    send_sem=idx_send.at[0], recv_sem=idx_recv.at[0],
                    device_id=at(xy, lax.rem(zc + k, SIDE)), device_id_type=MESH,
                ).start()
                return c

            lax.fori_loop(1, SIDE, share, 0)

        me = zc + q * (xy - zc)

        def send(k, c):
            to = lax.rem(me + k, SIDE)
            pltpu.make_async_remote_copy(
                src_ref=half.at[p, pl.ds(pl.multiple_of(to * SIDE, SIDE), SIDE)],
                dst_ref=recv.at[p, pl.ds(pl.multiple_of(me * SIDE, SIDE), SIDE)],
                send_sem=send1.at[p], recv_sem=recv1.at[p],
                device_id=at(xy + q * (to - xy), to + q * (zc - to)), device_id_type=MESH,
            ).start()
            return c

        lax.fori_loop(1, SIDE, send, 0)
        mine = pl.ds(pl.multiple_of(me * SIDE, SIDE), SIDE)
        recv[p, mine] = half[p, mine]
        return carry

    lax.fori_loop(0, PAIRS_HERE, phase1, 0)

    def got(ref, sem):
        pltpu.make_async_copy(ref, ref, sem).wait()

    def slab(ref, k):
        return ref.at[pl.ds(pl.multiple_of(k * SIDE, SIDE), SIDE)]

    def spread_out(src, dst, me, to_device, sends, recvs):
        def send(k, c):
            to = lax.rem(me + k, SIDE)
            pltpu.make_async_remote_copy(
                src_ref=slab(src, to), dst_ref=slab(dst, me), send_sem=sends, recv_sem=recvs,
                device_id=to_device(to), device_id_type=MESH,
            ).start()
            return c

        lax.fori_loop(1, SIDE, send, 0)
        slab(dst, me)[...] = slab(src, me)[...]

    def along_z(to):
        return at(xy, to)

    def along_xy(to):
        return at(to, zc)

    shift_row = iota((128, 128), 0)
    shift_col = iota((128, 128), 1)
    total = jnp.zeros((NOCC, 128), F32)
    for p in range(PAIRS_HERE):
        moved = dot(rest[p], one_hot((shift_col == shift_row + REST * p) & (shift_row < REST)), NN)
        if p % 2:
            moved = dot(perm[3], moved.astype(BF16), NN)
        total = total + moved
    rest_own[...] = total.astype(BF16)
    spread_out(rest_own, rest_recv, zc, along_z, rest_send.at[0], rest_sem.at[0])

    got(idx_z.at[0 : SIDE - 1], idx_recv.at[0])
    idx_zrow[...] = idx_z[:, 0, :]
    idx_all[xy] = idx_z[:, 0, :]

    def share2(k, c):
        pltpu.make_async_remote_copy(
            src_ref=idx_zrow, dst_ref=idx_all.at[xy],
            send_sem=idx_send.at[1], recv_sem=idx_recv.at[1],
            device_id=at(lax.rem(xy + k, SIDE), zc), device_id_type=MESH,
        ).start()
        return c

    lax.fori_loop(1, SIDE, share2, 0)
    got(idx_all.at[0 : SIDE - 1], idx_recv.at[1])

    lane_all = iota((NOCC, 128), 1)
    basis = iota((NOCC, NBP), 1)

    def build(p, c):
        table = idx_all[...].reshape(NOCC, 128).astype(F32)

        def chosen(j):
            return jnp.sum(jnp.where(lane_all == j, table, 0.0), axis=1, keepdims=True).astype(jnp.int32)

        lam = dot(one_hot(basis == chosen(2 * p)), occb[:, 0:128], NN)[:, 0:1]
        rows = dot(one_hot(basis == chosen(2 * p + 1)), virt[...], NT)
        kernel_rows = (lam * rows).astype(BF16)
        pk[p] = kernel_rows
        pkt[p] = dot(perm[2 + lax.rem(p, 2)], kernel_rows, NN).astype(BF16)
        return c

    lax.fori_loop(0, PAIRS_HERE, build, 0)

    def phase2(p):
        q = p % 2
        got(recv.at[p, 0 : (SIDE - 1) * SIDE], recv1.at[p])
        turned[p] = dot(perm[3], recv[p], NN).astype(BF16)
        if q == 0:
            spread_out(turned.at[p], final.at[p], xy, along_xy, send2.at[p], recv2.at[p])
        else:
            spread_out(turned.at[p], final.at[p], zc, along_z, send2.at[p], recv2.at[p])

    def phase2_rest():
        got(rest_recv.at[0 : (SIDE - 1) * SIDE], rest_sem.at[0])
        rest_turned[...] = dot(perm[3], rest_recv[...], NN).astype(BF16)
        spread_out(rest_turned, rest_final, xy, along_xy, rest_send.at[1], rest_sem.at[1])

    def add_rest():
        got(rest_final.at[0 : (SIDE - 1) * SIDE], rest_sem.at[1])
        total = jnp.zeros((REST, NVP), F32)
        for p in range(PAIRS_HERE):
            total = total + dot(rest_final[...], pk[p], TN)[REST * p : REST * (p + 1)]
        out[WIDE:NVIR] = (total[:, 0:NVIR] * SCALE).astype(BF16)

    def add(p, first=False, last=False):
        got(final.at[p, 0 : (SIDE - 1) * SIDE], recv2.at[p])
        for a0 in range(0, WIDE, 256):
            n = min(256, WIDE - a0)
            rows = pl.ds(a0, n)
            term = dot(final[p, :, rows], pkt[p], TN)
            if not first:
                term = acc[rows] + term
            if last:
                out[rows] = (term[:, 0:NVIR] * SCALE).astype(BF16)
            else:
                acc[rows] = term

    phase2(0)
    phase2(1)
    phase2(2)
    phase2_rest()
    add(0, first=True)
    phase2(3)
    add_rest()
    add(2)
    add(1)
    add(3, last=True)

    for p in range(PAIRS_HERE):
        got(half.at[p, 0 : (SIDE - 1) * SIDE], send1.at[p])
        got(turned.at[p, 0 : (SIDE - 1) * SIDE], send2.at[p])
    got(rest_own.at[0 : (SIDE - 1) * SIDE], rest_send.at[0])
    got(rest_turned.at[0 : (SIDE - 1) * SIDE], rest_send.at[1])
    got(idx_z.at[0 : SIDE - 1], idx_send.at[0])
    got(idx_all.at[0 : SIDE - 1], idx_send.at[1])


def shards(ao_slab, screen_mask, pair_ao, occ_coef, vir_coef):
    hbm = pl.BlockSpec(memory_space=pltpu.HBM)
    arrays = (ao_slab, screen_mask.transpose(1, 0, 2), pair_ao.T, occ_coef, vir_coef.T)
    dma = pltpu.SemaphoreType.DMA
    block = pl.pallas_call(
        kernel,
        name="mo_block",
        out_shape=pltpu.VMEM((NVIR, NVIR), BF16),
        in_specs=[hbm] * 5,
        out_specs=pl.BlockSpec(memory_space=pltpu.VMEM),
        scratch_shapes=[
            pltpu.VMEM((NBLK, PAIRS_HERE, NBLK), jnp.int32),
            pltpu.VMEM((2, PAIRS_HERE), jnp.int32),
            pltpu.VMEM((PAIRS_HERE, NBF, NBF), BF16),
            pltpu.VMEM((NBP, NOCC), BF16),
            pltpu.VMEM((NVIR, NBF), BF16),
            pltpu.VMEM((NVP, NBP), BF16),
            pltpu.VMEM((2, NOCC, NBP), BF16),
            pltpu.VMEM((4, NOCC, NOCC), BF16),
            pltpu.VMEM((PAIRS_HERE, 32, NBP), F32),
            pltpu.VMEM((NBP, NBP), BF16),
            pltpu.VMEM((NOCC, NBP), BF16),
            pltpu.VMEM((PAIRS_HERE, NOCC, WIDE), BF16),
            pltpu.VMEM((PAIRS_HERE, NOCC, WIDE), BF16),
            pltpu.VMEM((PAIRS_HERE, NOCC, WIDE), BF16),
            pltpu.VMEM((PAIRS_HERE, NOCC, WIDE), BF16),
            pltpu.VMEM((PAIRS_HERE, NOCC, 128), BF16),
            pltpu.VMEM((NOCC, 128), BF16),
            pltpu.VMEM((NOCC, 128), BF16),
            pltpu.VMEM((NOCC, 128), BF16),
            pltpu.VMEM((NOCC, 128), BF16),
            pltpu.VMEM((PAIRS_HERE, NOCC, NVP), BF16),
            pltpu.VMEM((PAIRS_HERE, NOCC, NVP), BF16),
            pltpu.VMEM((WIDE, NVP), F32),
            pltpu.VMEM((8, 128), jnp.int32),
            pltpu.VMEM((SIDE, 8, 128), jnp.int32),
            pltpu.VMEM((SIDE, 128), jnp.int32),
            pltpu.VMEM((SIDE, SIDE, 128), jnp.int32),
            dma((PAIRS_HERE,)),
            dma((4,)),
            dma((PAIRS_HERE,)),
            dma((PAIRS_HERE,)),
            dma((PAIRS_HERE,)),
            dma((PAIRS_HERE,)),
            dma((2,)),
            dma((2,)),
            dma((2,)),
            dma((2,)),
        ],
        compiler_params=pltpu.CompilerParams(
            collective_id=0, has_side_effects=True, vmem_limit_bytes=56 << 20
        ),
        cost_estimate=pl.CostEstimate(flops=7_000_000_000, bytes_accessed=16_000_000, transcendentals=0),
    )(*(pltpu.with_memory_space_constraint(x, pltpu.HBM) for x in arrays))
    return block.reshape(1, NVIR, 1, NVIR)


def solution(mesh):
    in_specs = (
        P(("grp", "wide"), None, None),
        P(("grp", "wide"), None, None),
        P(("grp", "wide"), None),
        P(),
        P(),
    )
    out_specs = P(("grp", "wide"), None, None, None)
    return jax.shard_map(shards, mesh=mesh, in_specs=in_specs, out_specs=out_specs, check_vma=False)
```

```python
import jax
import jax.numpy as jnp
from jax import lax
from jax.experimental import pallas as pl
from jax.experimental.pallas import tpu as pltpu
from jax.sharding import PartitionSpec as P

MESH = pl.DeviceIdType.MESH
BF16 = jnp.bfloat16
F32 = jnp.float32

NBF = 1200
NBP = 1280
NOCC = 256
NVIR = 900
NVP = 1024
WIDE = 896
REST = NVIR - WIDE
NBLK = 25
BLK = NBF // NBLK
PAIRS_HERE = 4
SIDE = 16
ORDER = (2, 14, 4, 12, 6, 10, 8, 3, 15, 5, 13, 7, 11, 9, 1)
PAIRS = 1024
SCALE = NBF / PAIRS**0.5
NN = (((1,), (0,)), ((), ()))
NT = (((1,), (1,)), ((), ()))
TN = (((0,), (0,)), ((), ()))


def dot(a, b, dims):
    return lax.dot_general(a, b, dims, preferred_element_type=F32)


def iota(shape, axis):
    return lax.broadcasted_iota(jnp.int32, shape, axis)


def one_hot(hit):
    return jnp.where(hit, 1.0, 0.0).astype(BF16)


def kernel(
    ao, mask, pair, occ, vir, out,
    mask_ref, pair_ref, aob, occb, virb, virt, occt, perm, mx, scr, left, half, recv, turned, final,
    rest, rest_own, rest_recv, rest_turned, rest_final, pk, pkt, acc,
    idx_own, idx_z, idx_zrow, idx_all,
    ao_sem, in_sem, send1, recv1, send2, recv2, rest_send, rest_sem, idx_send, idx_recv,
):
    grp = lax.axis_index("grp")
    wide = lax.axis_index("wide")
    zc = grp & (SIDE - 1)
    base = grp - zc
    xy = (grp >> 4) * 2 + wide

    def along_z(to):
        return (base + to, wide)

    def along_xy(to):
        return ((to >> 1) * SIDE + zc, to & 1)

    mask_copy = pltpu.make_async_copy(mask, mask_ref, in_sem.at[2])
    occ_copy = pltpu.make_async_copy(occ, occb.at[0:NBF], in_sem.at[0])
    vir_copy = pltpu.make_async_copy(vir, virb, in_sem.at[1])
    pair_copy = pltpu.make_async_copy(pair, pair_ref, in_sem.at[3])
    ao_copies = [pltpu.make_async_copy(ao.at[p], aob.at[p], ao_sem.at[p]) for p in range(PAIRS_HERE)]
    for copy in [mask_copy, occ_copy, ao_copies[0], vir_copy, pair_copy] + ao_copies[1:]:
        copy.start()

    barrier = pltpu.get_barrier_semaphore()
    for k in range(1, SIDE):
        for to in (along_z((zc + k) & (SIDE - 1)), along_xy((xy + k) & (SIDE - 1))):
            pl.semaphore_signal(barrier, inc=1, device_id=to, device_id_type=MESH)

    row = iota((NOCC, NOCC), 0)
    col = iota((NOCC, NOCC), 1)
    hi = lax.shift_right_logical(row, 4)
    lo = row & 15

    def owner(xy_of, zc_of):
        return (lax.shift_right_logical(xy_of, 1) * SIDE + zc_of) * 2 + (xy_of & 1)

    def spread_mask(p):
        block_of = iota((NBLK, NBP), 0) * BLK
        lane = iota((NBLK, NBP), 1)
        spread = one_hot((lane >= block_of) & (lane < block_of + BLK))
        mx[p, 0:NBLK] = dot(mask_ref[:, p, :].astype(F32).astype(BF16), spread, NN)

    scr[NBF:NBP, :] = jnp.zeros((NBP - NBF, NBP), BF16)
    scr[0:NBF, NBP - 128 : NBP] = jnp.zeros((NBF, 128), BF16)
    occb[NBF:NBP, :] = jnp.zeros((NBP - NBF, NOCC), BF16)
    virt[:, NBP - 128 : NBP] = jnp.zeros((NVP, 128), BF16)
    virt[WIDE:NVP, :] = jnp.zeros((NVP - WIDE, NBP), BF16)
    perm[0] = one_hot(col == owner(lo, hi))
    mask_copy.wait()
    spread_mask(0)
    occ_copy.wait()
    occt[0] = dot(perm[0], occb[...], NT).astype(BF16)

    def got(ref, sem):
        pltpu.make_async_copy(ref, ref, sem).wait()

    def slab(ref, k):
        return ref.at[pl.ds(pl.multiple_of(k * SIDE, SIDE), SIDE)]

    def spread_out(src, dst, me, to_device, sends, recvs, columns=slice(None)):
        for k in ORDER:
            to = (me + k) & (SIDE - 1)
            pltpu.make_async_remote_copy(
                src_ref=slab(src, to).at[:, columns], dst_ref=slab(dst, me).at[:, columns],
                send_sem=sends, recv_sem=recvs,
                device_id=to_device(to), device_id_type=MESH,
            ).start()
        slab(dst, me)[:, columns] = slab(src, me)[:, columns]

    def phase1(p, carry):
        q = p & 1
        pltpu.make_async_copy(ao.at[0], aob.at[p], ao_sem.at[p]).wait()

        def screen(r, c):
            rows = pl.ds(pl.multiple_of(r * BLK, BLK), BLK)
            keep = mx[p, pl.ds(r, 1), 0:NBF].astype(BF16)
            scr[rows, 0:NBF] = aob[p, rows, :] * keep
            return c

        lax.fori_loop(0, NBLK, screen, 0)
        left[...] = dot(occt[q], scr[...], NN).astype(BF16)

        @pl.when(p == 0)
        def _():
            vir_copy.wait()
            virt[0:NVIR, 0:NBF] = virb[...]

        both = dot(left[...], virt[...], NT)
        half[p] = both[:, 0:WIDE].astype(BF16)
        rest[p] = both[:, WIDE:NVP].astype(BF16)

        @pl.when(p == 0)
        def _():
            pl.semaphore_wait(barrier, 2 * (SIDE - 1))

        @pl.when(q == 0)
        def _():
            spread_out(half.at[p], recv.at[p], zc, along_z, send1.at[p], recv1.at[p])

        @pl.when(q == 1)
        def _():
            spread_out(half.at[p], recv.at[p], xy, along_xy, send1.at[p], recv1.at[p])

        @pl.when(p == 0)
        def _():
            pair_copy.wait()
            lane8 = iota((8, 128), 1)
            own = jnp.zeros((8, 128), jnp.int32)
            for pair_here in range(PAIRS_HERE):
                for j in range(2):
                    value = pair_ref[j : j + 1, pair_here : pair_here + 1]
                    own = jnp.where(lane8 == 2 * pair_here + j, value, own)
            idx_own[...] = own
            idx_z[zc] = own
            for k in range(1, SIDE):
                pltpu.make_async_remote_copy(
                    src_ref=idx_own, dst_ref=idx_z.at[zc],
                    send_sem=idx_send.at[0], recv_sem=idx_recv.at[0],
                    device_id=along_z((zc + k) & (SIDE - 1)), device_id_type=MESH,
                ).start()
            perm[1] = one_hot(col == owner(hi, lo))
            perm[2] = one_hot(col == row)
            perm[3] = one_hot(col == lo * SIDE + hi)
            for pair_here in range(1, PAIRS_HERE):
                spread_mask(pair_here)
            occt[1] = dot(perm[1], occb[...], NT).astype(BF16)

        return carry

    lax.fori_loop(0, PAIRS_HERE, phase1, 0)

    shift_row = iota((128, 128), 0)
    shift_col = iota((128, 128), 1)
    total = jnp.zeros((NOCC, 128), F32)
    for p in range(PAIRS_HERE):
        moved = dot(rest[p], one_hot((shift_col == shift_row + REST * p) & (shift_row < REST)), NN)
        if p % 2:
            moved = dot(perm[3], moved.astype(BF16), NN)
        total = total + moved
    rest_own[...] = total.astype(BF16)
    spread_out(rest_own, rest_recv, zc, along_z, rest_send.at[0], rest_sem.at[0])

    got(idx_z.at[0 : SIDE - 1], idx_recv.at[0])
    idx_zrow[...] = idx_z[:, 0, :]
    idx_all[xy] = idx_z[:, 0, :]

    for k in range(1, SIDE):
        pltpu.make_async_remote_copy(
            src_ref=idx_zrow, dst_ref=idx_all.at[xy],
            send_sem=idx_send.at[1], recv_sem=idx_recv.at[1],
            device_id=along_xy((xy + k) & (SIDE - 1)), device_id_type=MESH,
        ).start()

    lane_all = iota((NOCC, 128), 1)
    basis = iota((NOCC, NBP), 1)

    def build(p, c):
        table = idx_all[...].reshape(NOCC, 128).astype(F32)

        def chosen(j):
            return jnp.sum(jnp.where(lane_all == j, table, 0.0), axis=1, keepdims=True).astype(jnp.int32)

        lam = dot(one_hot(basis == chosen(2 * p)), occb[:, 0:128], NN)[:, 0:1]
        rows = dot(one_hot(basis == chosen(2 * p + 1)), virt[...], NT)
        kernel_rows = (lam * rows).astype(BF16)
        pk[p] = kernel_rows
        pkt[p] = dot(perm[2 + (p & 1)], kernel_rows, NN).astype(BF16)
        return c


    def phase2(p):
        got(recv.at[p, 0 : (SIDE - 1) * SIDE], recv1.at[p])
        turned[p] = dot(perm[3], recv[p], NN).astype(BF16)
        me, to_device = (zc, along_z) if p % 2 else (xy, along_xy)
        for part, columns in enumerate(parts_of(p)):
            spread_out(turned.at[p], final.at[p], me, to_device, send2.at[p], recv2.at[p, part], columns)

    def parts_of(p):
        return (slice(0, WIDE),)

    def phase2_rest():
        got(rest_recv.at[0 : (SIDE - 1) * SIDE], rest_sem.at[0])
        rest_turned[...] = dot(perm[3], rest_recv[...], NN).astype(BF16)
        spread_out(rest_turned, rest_final, xy, along_xy, rest_send.at[1], rest_sem.at[1])

    def add_rest():
        got(rest_final.at[0 : (SIDE - 1) * SIDE], rest_sem.at[1])
        total = jnp.zeros((REST, NVP), F32)
        for p in range(PAIRS_HERE):
            total = total + dot(rest_final[...], pk[p], TN)[REST * p : REST * (p + 1)]
        out[WIDE:NVIR] = (total[:, 0:NVIR] * SCALE).astype(BF16)

    def add(p, first=False, last=False):
        for part, columns in enumerate(parts_of(p)):
            got(final.at[p, 0 : (SIDE - 1) * SIDE, columns], recv2.at[p, part])
            for a0 in range(columns.start, columns.stop, 256):
                rows = pl.ds(a0, min(256, WIDE - a0))
                term = dot(final[p, :, rows], pkt[p], TN)
                if not first:
                    term = acc[rows] + term
                if last:
                    out[rows] = (term[:, 0:NVIR] * SCALE).astype(BF16)
                else:
                    acc[rows] = term

    phase2(0)
    phase2(1)
    got(idx_all.at[0 : SIDE - 1], idx_recv.at[1])
    lax.fori_loop(0, PAIRS_HERE, build, 0)
    phase2(2)
    phase2(3)
    phase2_rest()
    add(0, first=True)
    add(2)
    add_rest()
    add(1)
    add(3, last=True)

    for p in range(PAIRS_HERE):
        got(half.at[p, 0 : (SIDE - 1) * SIDE], send1.at[p])
        got(turned.at[p, 0 : (SIDE - 1) * SIDE], send2.at[p])
    got(rest_own.at[0 : (SIDE - 1) * SIDE], rest_send.at[0])
    got(rest_turned.at[0 : (SIDE - 1) * SIDE], rest_send.at[1])
    got(idx_z.at[0 : SIDE - 1], idx_send.at[0])
    got(idx_all.at[0 : SIDE - 1], idx_send.at[1])


def shards(ao_slab, screen_mask, pair_ao, occ_coef, vir_coef):
    hbm = pl.BlockSpec(memory_space=pltpu.HBM)
    arrays = (ao_slab, screen_mask.transpose(1, 0, 2), pair_ao.T, occ_coef, vir_coef.T)
    dma = pltpu.SemaphoreType.DMA
    block = pl.pallas_call(
        kernel,
        name="mo_block",
        out_shape=pltpu.VMEM((NVIR, NVIR), BF16),
        in_specs=[hbm] * 5,
        out_specs=pl.BlockSpec(memory_space=pltpu.VMEM),
        scratch_shapes=[
            pltpu.VMEM((NBLK, PAIRS_HERE, NBLK), jnp.int32),
            pltpu.VMEM((2, PAIRS_HERE), jnp.int32),
            pltpu.VMEM((PAIRS_HERE, NBF, NBF), BF16),
            pltpu.VMEM((NBP, NOCC), BF16),
            pltpu.VMEM((NVIR, NBF), BF16),
            pltpu.VMEM((NVP, NBP), BF16),
            pltpu.VMEM((2, NOCC, NBP), BF16),
            pltpu.VMEM((4, NOCC, NOCC), BF16),
            pltpu.VMEM((PAIRS_HERE, 32, NBP), F32),
            pltpu.VMEM((NBP, NBP), BF16),
            pltpu.VMEM((NOCC, NBP), BF16),
            pltpu.VMEM((PAIRS_HERE, NOCC, WIDE), BF16),
            pltpu.VMEM((PAIRS_HERE, NOCC, WIDE), BF16),
            pltpu.VMEM((PAIRS_HERE, NOCC, WIDE), BF16),
            pltpu.VMEM((PAIRS_HERE, NOCC, WIDE), BF16),
            pltpu.VMEM((PAIRS_HERE, NOCC, 128), BF16),
            pltpu.VMEM((NOCC, 128), BF16),
            pltpu.VMEM((NOCC, 128), BF16),
            pltpu.VMEM((NOCC, 128), BF16),
            pltpu.VMEM((NOCC, 128), BF16),
            pltpu.VMEM((PAIRS_HERE, NOCC, NVP), BF16),
            pltpu.VMEM((PAIRS_HERE, NOCC, NVP), BF16),
            pltpu.VMEM((WIDE, NVP), F32),
            pltpu.VMEM((8, 128), jnp.int32),
            pltpu.VMEM((SIDE, 8, 128), jnp.int32),
            pltpu.VMEM((SIDE, 128), jnp.int32),
            pltpu.VMEM((SIDE, SIDE, 128), jnp.int32),
            dma((PAIRS_HERE,)),
            dma((4,)),
            dma((PAIRS_HERE,)),
            dma((PAIRS_HERE,)),
            dma((PAIRS_HERE,)),
            dma((PAIRS_HERE, 2)),
            dma((2,)),
            dma((2,)),
            dma((2,)),
            dma((2,)),
        ],
        compiler_params=pltpu.CompilerParams(
            collective_id=0, has_side_effects=True, vmem_limit_bytes=56 << 20
        ),
        cost_estimate=pl.CostEstimate(flops=7_000_000_000, bytes_accessed=16_000_000, transcendentals=0),
    )(*(pltpu.with_memory_space_constraint(x, pltpu.HBM) for x in arrays))
    return block.reshape(1, NVIR, 1, NVIR)


def solution(mesh):
    in_specs = (
        P(("grp", "wide"), None, None),
        P(("grp", "wide"), None, None),
        P(("grp", "wide"), None),
        P(),
        P(),
    )
    out_specs = P(("grp", "wide"), None, None, None)
    return jax.shard_map(shards, mesh=mesh, in_specs=in_specs, out_specs=out_specs, check_vma=False)
```

```python
import jax
import jax.numpy as jnp
from jax import lax
from jax.experimental import pallas as pl
from jax.experimental.pallas import tpu as pltpu
from jax.sharding import PartitionSpec as P

MESH = pl.DeviceIdType.MESH
BF16 = jnp.bfloat16
F32 = jnp.float32

NBF = 1200
NBP = 1280
NOCC = 256
NVIR = 900
NVP = 1024
WIDE = 896
REST = NVIR - WIDE
NBLK = 25
BLK = NBF // NBLK
PAIRS_HERE = 4
SIDE = 16
ORDER = (2, 14, 4, 12, 6, 10, 8, 3, 15, 5, 13, 7, 11, 9, 1)
PAIRS = 1024
SCALE = NBF / PAIRS**0.5
NN = (((1,), (0,)), ((), ()))
NT = (((1,), (1,)), ((), ()))
TN = (((0,), (0,)), ((), ()))


def dot(a, b, dims):
    return lax.dot_general(a, b, dims, preferred_element_type=F32)


def iota(shape, axis):
    return lax.broadcasted_iota(jnp.int32, shape, axis)


def one_hot(hit):
    return jnp.where(hit, 1.0, 0.0).astype(BF16)


def kernel(
    ao, mask, pair, occ, vir, out,
    mask_ref, pair_ref, aob, occb, virb, virt, occt, perm, mx, scr, left, half, recv, turned, final,
    rest, rest_own, rest_z, rest_turned, rest_final, pk, pkt, acc,
    idx_own, idx_z, idx_zrow, idx_all,
    ao_sem, in_sem, send1, recv1, send2, recv2, rest_send, rest_sem, idx_send, idx_recv,
):
    grp = lax.axis_index("grp")
    wide = lax.axis_index("wide")
    zc = grp & (SIDE - 1)
    base = grp - zc
    xy = (grp >> 4) * 2 + wide

    def along_z(to):
        return (base + to, wide)

    def along_xy(to):
        return ((to >> 1) * SIDE + zc, to & 1)

    mask_copy = pltpu.make_async_copy(mask, mask_ref, in_sem.at[2])
    occ_copy = pltpu.make_async_copy(occ, occb.at[0:NBF], in_sem.at[0])
    vir_copy = pltpu.make_async_copy(vir, virb, in_sem.at[1])
    pair_copy = pltpu.make_async_copy(pair, pair_ref, in_sem.at[3])
    ao_copies = [pltpu.make_async_copy(ao.at[p], aob.at[p], ao_sem.at[p]) for p in range(PAIRS_HERE)]
    for copy in [mask_copy, occ_copy, ao_copies[0], vir_copy, pair_copy] + ao_copies[1:]:
        copy.start()

    barrier = pltpu.get_barrier_semaphore()
    for k in range(1, SIDE):
        for to in (along_z((zc + k) & (SIDE - 1)), along_xy((xy + k) & (SIDE - 1))):
            pl.semaphore_signal(barrier, inc=1, device_id=to, device_id_type=MESH)

    row = iota((NOCC, NOCC), 0)
    col = iota((NOCC, NOCC), 1)
    hi = lax.shift_right_logical(row, 4)
    lo = row & 15

    def owner(xy_of, zc_of):
        return (lax.shift_right_logical(xy_of, 1) * SIDE + zc_of) * 2 + (xy_of & 1)

    def spread_mask(p):
        block_of = iota((NBLK, NBP), 0) * BLK
        lane = iota((NBLK, NBP), 1)
        spread = one_hot((lane >= block_of) & (lane < block_of + BLK))
        mx[p, 0:NBLK] = dot(mask_ref[:, p, :].astype(F32).astype(BF16), spread, NN)

    scr[NBF:NBP, :] = jnp.zeros((NBP - NBF, NBP), BF16)
    scr[0:NBF, NBP - 128 : NBP] = jnp.zeros((NBF, 128), BF16)
    occb[NBF:NBP, :] = jnp.zeros((NBP - NBF, NOCC), BF16)
    virt[:, NBP - 128 : NBP] = jnp.zeros((NVP, 128), BF16)
    virt[WIDE:NVP, :] = jnp.zeros((NVP - WIDE, NBP), BF16)
    perm[0] = one_hot(col == owner(lo, hi))
    mask_copy.wait()
    spread_mask(0)
    occ_copy.wait()
    occt[0] = dot(perm[0], occb[...], NT).astype(BF16)

    def got(ref, sem):
        pltpu.make_async_copy(ref, ref, sem).wait()

    def slab(ref, k):
        return ref.at[pl.ds(pl.multiple_of(k * SIDE, SIDE), SIDE)]

    def spread_out(src, dst, me, to_device, sends, recvs, columns=slice(None)):
        for k in ORDER:
            to = (me + k) & (SIDE - 1)
            pltpu.make_async_remote_copy(
                src_ref=slab(src, to).at[:, columns], dst_ref=slab(dst, me).at[:, columns],
                send_sem=sends, recv_sem=recvs,
                device_id=to_device(to), device_id_type=MESH,
            ).start()
        slab(dst, me)[:, columns] = slab(src, me)[:, columns]

    def phase1(p, carry):
        q = p & 1
        pltpu.make_async_copy(ao.at[0], aob.at[p], ao_sem.at[p]).wait()

        def screen(r, c):
            rows = pl.ds(pl.multiple_of(r * BLK, BLK), BLK)
            keep = mx[p, pl.ds(r, 1), 0:NBF].astype(BF16)
            scr[rows, 0:NBF] = aob[p, rows, :] * keep
            return c

        lax.fori_loop(0, NBLK, screen, 0)
        left[...] = dot(occt[q], scr[...], NN).astype(BF16)

        @pl.when(p == 0)
        def _():
            vir_copy.wait()
            virt[0:NVIR, 0:NBF] = virb[...]

        both = dot(left[...], virt[...], NT)
        half[p] = both[:, 0:WIDE].astype(BF16)
        rest[p] = both[:, WIDE:NVP].astype(BF16)

        @pl.when(p == 0)
        def _():
            pl.semaphore_wait(barrier, 2 * (SIDE - 1))

        @pl.when(q == 0)
        def _():
            spread_out(half.at[p], recv.at[p], zc, along_z, send1.at[p], recv1.at[p])

        @pl.when(q == 1)
        def _():
            spread_out(half.at[p], recv.at[p], xy, along_xy, send1.at[p], recv1.at[p])

        @pl.when(p == 0)
        def _():
            pair_copy.wait()
            lane_own = iota((1, 128), 1)
            own = jnp.zeros((1, 128), jnp.int32)
            for pair_here in range(PAIRS_HERE):
                for j in range(2):
                    value = pair_ref[j : j + 1, pair_here : pair_here + 1]
                    own = jnp.where(lane_own == 2 * pair_here + j, value, own)
            idx_own[...] = own
            idx_z[zc] = own
            for k in range(1, SIDE):
                pltpu.make_async_remote_copy(
                    src_ref=idx_own, dst_ref=idx_z.at[zc],
                    send_sem=idx_send.at[0], recv_sem=idx_recv.at[0],
                    device_id=along_z((zc + k) & (SIDE - 1)), device_id_type=MESH,
                ).start()
            perm[1] = one_hot(col == owner(hi, lo))
            perm[2] = one_hot(col == row)
            perm[3] = one_hot(col == lo * SIDE + hi)
            for pair_here in range(1, PAIRS_HERE):
                spread_mask(pair_here)
            occt[1] = dot(perm[1], occb[...], NT).astype(BF16)

        return carry

    lax.fori_loop(0, PAIRS_HERE, phase1, 0)

    lane_row = iota((128, 128), 0)
    lane_col = iota((128, 128), 1)
    total = jnp.zeros((NOCC, 128), F32)
    for p in range(PAIRS_HERE):
        moved = dot(rest[p], one_hot(((lane_col & 15) == lane_row + REST * p) & (lane_row < REST)), NN)
        if p % 2:
            moved = dot(perm[3], moved.astype(BF16), NN)
        total = total + moved
    rest_row = iota((NOCC, 128), 0)
    in_group = lax.shift_right_logical(iota((NOCC, 128), 1), 4) == (rest_row & 7)
    low_half = (rest_row & 8) == 0
    picked = jnp.where(in_group, total, 0.0).astype(BF16)
    fold_row = iota((SIDE, NOCC), 0)
    fold_col = iota((SIDE, NOCC), 1)
    for h in range(2):
        fold = (lax.shift_right_logical(fold_col, 4) == fold_row) & ((fold_col & 8) == 8 * h)
        rest_own[:, h, :] = dot(one_hot(fold), picked, NN)
    rest_z[zc] = rest_own[zc]
    for k in ORDER:
        to = (zc + k) & (SIDE - 1)
        pltpu.make_async_remote_copy(
            src_ref=rest_own.at[to], dst_ref=rest_z.at[zc],
            send_sem=rest_send.at[0], recv_sem=rest_sem.at[0],
            device_id=along_z(to), device_id_type=MESH,
        ).start()

    got(idx_z.at[0 : SIDE - 1], idx_recv.at[0])
    idx_zrow[...] = idx_z[:, 0, :]
    idx_all[xy] = idx_z[:, 0, :]

    for k in range(1, SIDE):
        pltpu.make_async_remote_copy(
            src_ref=idx_zrow, dst_ref=idx_all.at[xy],
            send_sem=idx_send.at[1], recv_sem=idx_recv.at[1],
            device_id=along_xy((xy + k) & (SIDE - 1)), device_id_type=MESH,
        ).start()

    lane_all = iota((NOCC, 128), 1)
    basis = iota((NOCC, NBP), 1)

    def build(p, c):
        table = idx_all[...].reshape(NOCC, 128).astype(F32)

        def chosen(j):
            return jnp.sum(jnp.where(lane_all == j, table, 0.0), axis=1, keepdims=True).astype(jnp.int32)

        lam = dot(one_hot(basis == chosen(2 * p)), occb[:, 0:128], NN)[:, 0:1]
        rows = dot(one_hot(basis == chosen(2 * p + 1)), virt[...], NT)
        kernel_rows = (lam * rows).astype(BF16)
        pk[p] = kernel_rows
        pkt[p] = dot(perm[2 + (p & 1)], kernel_rows, NN).astype(BF16)
        return c


    def phase2(p):
        got(recv.at[p, 0 : (SIDE - 1) * SIDE], recv1.at[p])
        turned[p] = dot(perm[3], recv[p], NN).astype(BF16)
        me, to_device = (zc, along_z) if p % 2 else (xy, along_xy)
        for part, columns in enumerate(parts_of(p)):
            spread_out(turned.at[p], final.at[p], me, to_device, send2.at[p], recv2.at[p, part], columns)

    def parts_of(p):
        return (slice(0, 512), slice(512, WIDE)) if p == PAIRS_HERE - 1 else (slice(0, WIDE),)

    def phase2_rest():
        got(rest_z.at[0 : SIDE - 1], rest_sem.at[0])
        source = one_hot(lax.shift_right_logical(iota((NOCC, SIDE), 0), 4) == iota((NOCC, SIDE), 1))
        halves = [dot(source, rest_z[:, h, :].astype(BF16), NN) for h in range(2)]
        unfolded = jnp.where(in_group, jnp.where(low_half, halves[0], halves[1]), 0.0).astype(BF16)
        unfold = one_hot(((lane_row & 15) == lane_col) & (lane_col < SIDE))
        received = dot(unfolded, unfold, NN).astype(BF16)
        rest_turned[...] = dot(perm[3], received, NN).astype(BF16)
        spread_out(rest_turned, rest_final, xy, along_xy, rest_send.at[1], rest_sem.at[1])

    def add_rest():
        got(rest_final.at[0 : (SIDE - 1) * SIDE], rest_sem.at[1])
        total = jnp.zeros((REST, NVP), F32)
        for p in range(PAIRS_HERE):
            total = total + dot(rest_final[...], pk[p], TN)[REST * p : REST * (p + 1)]
        out[WIDE:NVIR] = (total[:, 0:NVIR] * SCALE).astype(BF16)

    def add(p, first=False, last=False):
        for part, columns in enumerate(parts_of(p)):
            got(final.at[p, 0 : (SIDE - 1) * SIDE, columns], recv2.at[p, part])
            for a0 in range(columns.start, columns.stop, 256):
                rows = pl.ds(a0, min(256, WIDE - a0))
                term = dot(final[p, :, rows], pkt[p], TN)
                if not first:
                    term = acc[rows] + term
                if last:
                    out[rows] = (term[:, 0:NVIR] * SCALE).astype(BF16)
                else:
                    acc[rows] = term

    phase2(0)
    phase2(1)
    phase2(2)
    phase2(3)
    phase2_rest()
    got(idx_all.at[0 : SIDE - 1], idx_recv.at[1])
    lax.fori_loop(0, PAIRS_HERE, build, 0)
    add(0, first=True)
    add(2)
    add_rest()
    add(1)
    add(3, last=True)

    for p in range(PAIRS_HERE):
        got(half.at[p, 0 : (SIDE - 1) * SIDE], send1.at[p])
        got(turned.at[p, 0 : (SIDE - 1) * SIDE], send2.at[p])
    got(rest_own.at[0 : SIDE - 1], rest_send.at[0])
    got(rest_turned.at[0 : (SIDE - 1) * SIDE], rest_send.at[1])
    got(idx_z.at[0 : SIDE - 1], idx_send.at[0])
    got(idx_all.at[0 : SIDE - 1], idx_send.at[1])


def shards(ao_slab, screen_mask, pair_ao, occ_coef, vir_coef):
    hbm = pl.BlockSpec(memory_space=pltpu.HBM)
    arrays = (ao_slab, screen_mask.transpose(1, 0, 2), pair_ao.T, occ_coef, vir_coef.T)
    dma = pltpu.SemaphoreType.DMA
    block = pl.pallas_call(
        kernel,
        name="mo_block",
        out_shape=pltpu.VMEM((NVIR, NVIR), BF16),
        in_specs=[hbm] * 5,
        out_specs=pl.BlockSpec(memory_space=pltpu.VMEM),
        scratch_shapes=[
            pltpu.VMEM((NBLK, PAIRS_HERE, NBLK), jnp.int32),
            pltpu.VMEM((2, PAIRS_HERE), jnp.int32),
            pltpu.VMEM((PAIRS_HERE, NBF, NBF), BF16),
            pltpu.VMEM((NBP, NOCC), BF16),
            pltpu.VMEM((NVIR, NBF), BF16),
            pltpu.VMEM((NVP, NBP), BF16),
            pltpu.VMEM((2, NOCC, NBP), BF16),
            pltpu.VMEM((4, NOCC, NOCC), BF16),
            pltpu.VMEM((PAIRS_HERE, 32, NBP), F32),
            pltpu.VMEM((NBP, NBP), BF16),
            pltpu.VMEM((NOCC, NBP), BF16),
            pltpu.VMEM((PAIRS_HERE, NOCC, WIDE), BF16),
            pltpu.VMEM((PAIRS_HERE, NOCC, WIDE), BF16),
            pltpu.VMEM((PAIRS_HERE, NOCC, WIDE), BF16),
            pltpu.VMEM((PAIRS_HERE, NOCC, WIDE), BF16),
            pltpu.VMEM((PAIRS_HERE, NOCC, 128), BF16),
            pltpu.VMEM((SIDE, 2, 128), F32),
            pltpu.VMEM((SIDE, 2, 128), F32),
            pltpu.VMEM((NOCC, 128), BF16),
            pltpu.VMEM((NOCC, 128), BF16),
            pltpu.VMEM((PAIRS_HERE, NOCC, NVP), BF16),
            pltpu.VMEM((PAIRS_HERE, NOCC, NVP), BF16),
            pltpu.VMEM((WIDE, NVP), F32),
            pltpu.VMEM((1, 128), jnp.int32),
            pltpu.VMEM((SIDE, 1, 128), jnp.int32),
            pltpu.VMEM((SIDE, 128), jnp.int32),
            pltpu.VMEM((SIDE, SIDE, 128), jnp.int32),
            dma((PAIRS_HERE,)),
            dma((4,)),
            dma((PAIRS_HERE,)),
            dma((PAIRS_HERE,)),
            dma((PAIRS_HERE,)),
            dma((PAIRS_HERE, 2)),
            dma((2,)),
            dma((2,)),
            dma((2,)),
            dma((2,)),
        ],
        compiler_params=pltpu.CompilerParams(
            collective_id=0, has_side_effects=True, vmem_limit_bytes=56 << 20
        ),
        cost_estimate=pl.CostEstimate(flops=7_000_000_000, bytes_accessed=16_000_000, transcendentals=0),
    )(*(pltpu.with_memory_space_constraint(x, pltpu.HBM) for x in arrays))
    return block.reshape(1, NVIR, 1, NVIR)


def solution(mesh):
    in_specs = (
        P(("grp", "wide"), None, None),
        P(("grp", "wide"), None, None),
        P(("grp", "wide"), None),
        P(),
        P(),
    )
    out_specs = P(("grp", "wide"), None, None, None)
    return jax.shard_map(shards, mesh=mesh, in_specs=in_specs, out_specs=out_specs, check_vma=False)
```

```python
import jax
import jax.numpy as jnp
from jax import lax
from jax.experimental import pallas as pl
from jax.experimental.pallas import tpu as pltpu
from jax.sharding import PartitionSpec as P

MESH = pl.DeviceIdType.MESH
BF16 = jnp.bfloat16
F32 = jnp.float32

NBF = 1200
NBP = 1280
NOCC = 256
NVIR = 900
NVP = 1024
WIDE = 896
REST = NVIR - WIDE
NBLK = 25
BLK = NBF // NBLK
PAIRS_HERE = 4
SIDE = 16
ORDER = (8, 9, 6, 10, 7, 11, 4, 12, 5, 13, 2, 14, 3, 15, 1)
PAIRS = 1024
SCALE = NBF / PAIRS**0.5
NN = (((1,), (0,)), ((), ()))
NT = (((1,), (1,)), ((), ()))
TN = (((0,), (0,)), ((), ()))


def dot(a, b, dims):
    return lax.dot_general(a, b, dims, preferred_element_type=F32)


def iota(shape, axis):
    return lax.broadcasted_iota(jnp.int32, shape, axis)


def one_hot(hit):
    return jnp.where(hit, 1.0, 0.0).astype(BF16)


def kernel(
    ao, mask, pair, occ, vir, out,
    mask_ref, pair_ref, aob, occb, virb, virt, occt, perm, mx, scr, left, half, recv, turned, final,
    rest, rest_own, rest_z, rest_turned, rest_final, pk, pkt, acc,
    idx_own, idx_z, idx_zrow, idx_all,
    ao_sem, in_sem, send1, recv1, send2, recv2, rest_send, rest_sem, idx_send, idx_recv,
):
    grp = lax.axis_index("grp")
    wide = lax.axis_index("wide")
    zc = grp & (SIDE - 1)
    base = grp - zc
    xy = (grp >> 4) * 2 + wide

    def along_z(to):
        return (base + to, wide)

    def along_xy(to):
        return ((to >> 1) * SIDE + zc, to & 1)

    mask_copy = pltpu.make_async_copy(mask, mask_ref, in_sem.at[2])
    occ_copy = pltpu.make_async_copy(occ, occb.at[0:NBF], in_sem.at[0])
    vir_copy = pltpu.make_async_copy(vir, virb, in_sem.at[1])
    pair_copy = pltpu.make_async_copy(pair, pair_ref, in_sem.at[3])

    def ao_copy(p):
        return pltpu.make_async_copy(ao.at[p], aob.at[p], ao_sem.at[p])

    for copy in (mask_copy, occ_copy, ao_copy(0), vir_copy, pair_copy):
        copy.start()

    barrier = pltpu.get_barrier_semaphore()
    for k in range(1, SIDE):
        for to in (along_z((zc + k) & (SIDE - 1)), along_xy((xy + k) & (SIDE - 1))):
            pl.semaphore_signal(barrier, inc=1, device_id=to, device_id_type=MESH)

    row = iota((NOCC, NOCC), 0)
    col = iota((NOCC, NOCC), 1)
    hi = lax.shift_right_logical(row, 4)
    lo = row & 15

    def owner(xy_of, zc_of):
        return (lax.shift_right_logical(xy_of, 1) * SIDE + zc_of) * 2 + (xy_of & 1)

    def spread_mask(p):
        block_of = iota((NBLK, NBP), 0) * BLK
        lane = iota((NBLK, NBP), 1)
        spread = one_hot((lane >= block_of) & (lane < block_of + BLK))
        mx[p, 0:NBLK] = dot(mask_ref[:, p, :].astype(F32).astype(BF16), spread, NN)

    scr[NBF:NBP, :] = jnp.zeros((NBP - NBF, NBP), BF16)
    scr[0:NBF, NBP - 128 : NBP] = jnp.zeros((NBF, 128), BF16)
    occb[NBF:NBP, :] = jnp.zeros((NBP - NBF, NOCC), BF16)
    virt[:, NBP - 128 : NBP] = jnp.zeros((NVP, 128), BF16)
    virt[WIDE:NVP, :] = jnp.zeros((NVP - WIDE, NBP), BF16)
    perm[0] = one_hot(col == owner(lo, hi))
    mask_copy.wait()
    spread_mask(0)
    occ_copy.wait()
    occt[0] = dot(perm[0], occb[...], NT).astype(BF16)

    def got(ref, sem):
        pltpu.make_async_copy(ref, ref, sem).wait()

    def slab(ref, k):
        return ref.at[pl.ds(pl.multiple_of(k * SIDE, SIDE), SIDE)]

    def spread_out(src, dst, me, to_device, sends, recvs, columns=slice(None)):
        for k in ORDER:
            to = (me + k) & (SIDE - 1)
            pltpu.make_async_remote_copy(
                src_ref=slab(src, to).at[:, columns], dst_ref=slab(dst, me).at[:, columns],
                send_sem=sends, recv_sem=recvs,
                device_id=to_device(to), device_id_type=MESH,
            ).start()
        slab(dst, me)[:, columns] = slab(src, me)[:, columns]

    def phase1(p, carry):
        q = p & 1
        ao_copy(p).wait()

        @pl.when(p < PAIRS_HERE - 1)
        def _():
            ao_copy(p + 1).start()


        def screen(r, c):
            rows = pl.ds(pl.multiple_of(r * BLK, BLK), BLK)
            keep = mx[p, pl.ds(r, 1), 0:NBF].astype(BF16)
            scr[rows, 0:NBF] = aob[p, rows, :] * keep
            return c

        lax.fori_loop(0, NBLK, screen, 0)
        left[...] = dot(occt[q], scr[...], NN).astype(BF16)

        @pl.when(p == 0)
        def _():
            vir_copy.wait()
            virt[0:NVIR, 0:NBF] = virb[...]

        both = dot(left[...], virt[...], NT)
        half[p] = both[:, 0:WIDE].astype(BF16)
        rest[p] = both[:, WIDE:NVP].astype(BF16)

        @pl.when(p == 0)
        def _():
            pl.semaphore_wait(barrier, 2 * (SIDE - 1))

        @pl.when(q == 0)
        def _():
            spread_out(half.at[p], recv.at[p], zc, along_z, send1.at[p], recv1.at[p])

        @pl.when(q == 1)
        def _():
            spread_out(half.at[p], recv.at[p], xy, along_xy, send1.at[p], recv1.at[p])

        @pl.when(p == 0)
        def _():
            pair_copy.wait()
            lane_own = iota((1, 128), 1)
            own = jnp.zeros((1, 128), jnp.int32)
            for pair_here in range(PAIRS_HERE):
                for j in range(2):
                    value = pair_ref[j : j + 1, pair_here : pair_here + 1]
                    own = jnp.where(lane_own == 2 * pair_here + j, value, own)
            idx_own[...] = own
            idx_z[zc] = own
            for k in range(1, SIDE):
                pltpu.make_async_remote_copy(
                    src_ref=idx_own, dst_ref=idx_z.at[zc],
                    send_sem=idx_send.at[0], recv_sem=idx_recv.at[0],
                    device_id=along_z((zc + k) & (SIDE - 1)), device_id_type=MESH,
                ).start()
            perm[1] = one_hot(col == owner(hi, lo))
            perm[2] = one_hot(col == row)
            perm[3] = one_hot(col == lo * SIDE + hi)
            for pair_here in range(1, PAIRS_HERE):
                spread_mask(pair_here)
            occt[1] = dot(perm[1], occb[...], NT).astype(BF16)

        return carry

    lax.fori_loop(0, PAIRS_HERE, phase1, 0)

    lane_row = iota((128, 128), 0)
    lane_col = iota((128, 128), 1)
    total = jnp.zeros((NOCC, 128), F32)
    for p in range(PAIRS_HERE):
        moved = dot(rest[p], one_hot(((lane_col & 15) == lane_row + REST * p) & (lane_row < REST)), NN)
        if p % 2:
            moved = dot(perm[3], moved.astype(BF16), NN)
        total = total + moved
    rest_row = iota((NOCC, 128), 0)
    in_group = lax.shift_right_logical(iota((NOCC, 128), 1), 4) == (rest_row & 7)
    low_half = (rest_row & 8) == 0
    picked = jnp.where(in_group, total, 0.0).astype(BF16)
    fold_row = iota((SIDE, NOCC), 0)
    fold_col = iota((SIDE, NOCC), 1)
    for h in range(2):
        fold = (lax.shift_right_logical(fold_col, 4) == fold_row) & ((fold_col & 8) == 8 * h)
        rest_own[:, h, :] = dot(one_hot(fold), picked, NN)
    rest_z[zc] = rest_own[zc]
    for k in ORDER:
        to = (zc + k) & (SIDE - 1)
        pltpu.make_async_remote_copy(
            src_ref=rest_own.at[to], dst_ref=rest_z.at[zc],
            send_sem=rest_send.at[0], recv_sem=rest_sem.at[0],
            device_id=along_z(to), device_id_type=MESH,
        ).start()

    got(idx_z.at[0 : SIDE - 1], idx_recv.at[0])
    idx_zrow[...] = idx_z[:, 0, :]
    idx_all[xy] = idx_z[:, 0, :]

    for k in range(1, SIDE):
        pltpu.make_async_remote_copy(
            src_ref=idx_zrow, dst_ref=idx_all.at[xy],
            send_sem=idx_send.at[1], recv_sem=idx_recv.at[1],
            device_id=along_xy((xy + k) & (SIDE - 1)), device_id_type=MESH,
        ).start()

    lane_all = iota((NOCC, 128), 1)
    basis = iota((NOCC, NBP), 1)

    def build(p, c):
        table = idx_all[...].reshape(NOCC, 128).astype(F32)

        def chosen(j):
            return jnp.sum(jnp.where(lane_all == j, table, 0.0), axis=1, keepdims=True).astype(jnp.int32)

        lam = dot(one_hot(basis == chosen(2 * p)), occb[:, 0:128], NN)[:, 0:1]
        rows = dot(one_hot(basis == chosen(2 * p + 1)), virt[...], NT)
        kernel_rows = (lam * rows).astype(BF16)
        pk[p] = kernel_rows
        pkt[p] = dot(perm[2 + (p & 1)], kernel_rows, NN).astype(BF16)
        return c


    def phase2(p):
        got(recv.at[p, 0 : (SIDE - 1) * SIDE], recv1.at[p])
        turned[p] = dot(perm[3], recv[p], NN).astype(BF16)
        me, to_device = (zc, along_z) if p % 2 else (xy, along_xy)
        for part, columns in enumerate(parts_of(p)):
            spread_out(turned.at[p], final.at[p], me, to_device, send2.at[p], recv2.at[p, part], columns)

    def parts_of(p):
        return (slice(0, 512), slice(512, WIDE)) if p == PAIRS_HERE - 1 else (slice(0, WIDE),)

    def phase2_rest():
        got(rest_z.at[0 : SIDE - 1], rest_sem.at[0])
        source = one_hot(lax.shift_right_logical(iota((NOCC, SIDE), 0), 4) == iota((NOCC, SIDE), 1))
        halves = [dot(source, rest_z[:, h, :].astype(BF16), NN) for h in range(2)]
        unfolded = jnp.where(in_group, jnp.where(low_half, halves[0], halves[1]), 0.0).astype(BF16)
        unfold = one_hot(((lane_row & 15) == lane_col) & (lane_col < SIDE))
        received = dot(unfolded, unfold, NN).astype(BF16)
        rest_turned[...] = dot(perm[3], received, NN).astype(BF16)
        spread_out(rest_turned, rest_final, xy, along_xy, rest_send.at[1], rest_sem.at[1])

    def add_rest():
        got(rest_final.at[0 : (SIDE - 1) * SIDE], rest_sem.at[1])
        total = jnp.zeros((REST, NVP), F32)
        for p in range(PAIRS_HERE):
            total = total + dot(rest_final[...], pk[p], TN)[REST * p : REST * (p + 1)]
        out[WIDE:NVIR] = (total[:, 0:NVIR] * SCALE).astype(BF16)

    def add(p, first=False, last=False):
        for part, columns in enumerate(parts_of(p)):
            got(final.at[p, 0 : (SIDE - 1) * SIDE, columns], recv2.at[p, part])
            for a0 in range(columns.start, columns.stop, 256):
                rows = pl.ds(a0, min(256, WIDE - a0))
                term = dot(final[p, :, rows], pkt[p], TN)
                if not first:
                    term = acc[rows] + term
                if last:
                    out[rows] = (term[:, 0:NVIR] * SCALE).astype(BF16)
                else:
                    acc[rows] = term

    phase2(0)
    phase2(1)
    phase2(2)
    phase2(3)
    phase2_rest()
    got(idx_all.at[0 : SIDE - 1], idx_recv.at[1])
    lax.fori_loop(0, PAIRS_HERE, build, 0)
    add(0, first=True)
    add(2)
    add_rest()
    add(1)
    add(3, last=True)

    for p in range(PAIRS_HERE):
        got(half.at[p, 0 : (SIDE - 1) * SIDE], send1.at[p])
        got(turned.at[p, 0 : (SIDE - 1) * SIDE], send2.at[p])
    got(rest_own.at[0 : SIDE - 1], rest_send.at[0])
    got(rest_turned.at[0 : (SIDE - 1) * SIDE], rest_send.at[1])
    got(idx_z.at[0 : SIDE - 1], idx_send.at[0])
    got(idx_all.at[0 : SIDE - 1], idx_send.at[1])


def shards(ao_slab, screen_mask, pair_ao, occ_coef, vir_coef):
    hbm = pl.BlockSpec(memory_space=pltpu.HBM)
    arrays = (ao_slab, screen_mask.transpose(1, 0, 2), pair_ao.T, occ_coef, vir_coef.T)
    dma = pltpu.SemaphoreType.DMA
    block = pl.pallas_call(
        kernel,
        name="mo_block",
        out_shape=pltpu.VMEM((NVIR, NVIR), BF16),
        in_specs=[hbm] * 5,
        out_specs=pl.BlockSpec(memory_space=pltpu.VMEM),
        scratch_shapes=[
            pltpu.VMEM((NBLK, PAIRS_HERE, NBLK), jnp.int32),
            pltpu.VMEM((2, PAIRS_HERE), jnp.int32),
            pltpu.VMEM((PAIRS_HERE, NBF, NBF), BF16),
            pltpu.VMEM((NBP, NOCC), BF16),
            pltpu.VMEM((NVIR, NBF), BF16),
            pltpu.VMEM((NVP, NBP), BF16),
            pltpu.VMEM((2, NOCC, NBP), BF16),
            pltpu.VMEM((4, NOCC, NOCC), BF16),
            pltpu.VMEM((PAIRS_HERE, 32, NBP), F32),
            pltpu.VMEM((NBP, NBP), BF16),
            pltpu.VMEM((NOCC, NBP), BF16),
            pltpu.VMEM((PAIRS_HERE, NOCC, WIDE), BF16),
            pltpu.VMEM((PAIRS_HERE, NOCC, WIDE), BF16),
            pltpu.VMEM((PAIRS_HERE, NOCC, WIDE), BF16),
            pltpu.VMEM((PAIRS_HERE, NOCC, WIDE), BF16),
            pltpu.VMEM((PAIRS_HERE, NOCC, 128), BF16),
            pltpu.VMEM((SIDE, 2, 128), F32),
            pltpu.VMEM((SIDE, 2, 128), F32),
            pltpu.VMEM((NOCC, 128), BF16),
            pltpu.VMEM((NOCC, 128), BF16),
            pltpu.VMEM((PAIRS_HERE, NOCC, NVP), BF16),
            pltpu.VMEM((PAIRS_HERE, NOCC, NVP), BF16),
            pltpu.VMEM((WIDE, NVP), F32),
            pltpu.VMEM((1, 128), jnp.int32),
            pltpu.VMEM((SIDE, 1, 128), jnp.int32),
            pltpu.VMEM((SIDE, 128), jnp.int32),
            pltpu.VMEM((SIDE, SIDE, 128), jnp.int32),
            dma((PAIRS_HERE,)),
            dma((4,)),
            dma((PAIRS_HERE,)),
            dma((PAIRS_HERE,)),
            dma((PAIRS_HERE,)),
            dma((PAIRS_HERE, 2)),
            dma((2,)),
            dma((2,)),
            dma((2,)),
            dma((2,)),
        ],
        compiler_params=pltpu.CompilerParams(
            collective_id=0, has_side_effects=True, vmem_limit_bytes=56 << 20
        ),
        cost_estimate=pl.CostEstimate(flops=7_000_000_000, bytes_accessed=16_000_000, transcendentals=0),
    )(*(pltpu.with_memory_space_constraint(x, pltpu.HBM) for x in arrays))
    return block.reshape(1, NVIR, 1, NVIR)


def solution(mesh):
    in_specs = (
        P(("grp", "wide"), None, None),
        P(("grp", "wide"), None, None),
        P(("grp", "wide"), None),
        P(),
        P(),
    )
    out_specs = P(("grp", "wide"), None, None, None)
    return jax.shard_map(shards, mesh=mesh, in_specs=in_specs, out_specs=out_specs, check_vma=False)
```

```python
import jax
import jax.numpy as jnp
from jax import lax
from jax.experimental import pallas as pl
from jax.experimental.pallas import tpu as pltpu
from jax.sharding import PartitionSpec as P

MESH = pl.DeviceIdType.MESH
BF16 = jnp.bfloat16
F32 = jnp.float32

NBF = 1200
NBP = 1280
NOCC = 256
NVIR = 900
NVP = 1024
WIDE = 896
REST = NVIR - WIDE
NBLK = 25
BLK = NBF // NBLK
PAIRS_HERE = 4
SIDE = 16
ORDER = (8, 9, 6, 10, 7, 11, 4, 12, 5, 13, 2, 14, 3, 15, 1)
PAIRS = 1024
SCALE = NBF / PAIRS**0.5
NN = (((1,), (0,)), ((), ()))
NT = (((1,), (1,)), ((), ()))
TN = (((0,), (0,)), ((), ()))


def dot(a, b, dims):
    return lax.dot_general(a, b, dims, preferred_element_type=F32)


def iota(shape, axis):
    return lax.broadcasted_iota(jnp.int32, shape, axis)


def one_hot(hit):
    return jnp.where(hit, 1.0, 0.0).astype(BF16)


def kernel(
    ao, mask, pair, occ, vir, out,
    mask_ref, pair_ref, aob, occb, virb, virt, occt, perm, mx, scr, left, half, recv, turned, final,
    rest, rest_own, rest_z, rest_turned, rest_final, pk, pkt, acc,
    idx_own, idx_z, idx_zrow, idx_all,
    ao_sem, in_sem, send1, recv1, send2, recv2, rest_send, rest_sem, idx_send, idx_recv,
):
    grp = lax.axis_index("grp")
    wide = lax.axis_index("wide")
    zc = grp & (SIDE - 1)
    base = grp - zc
    xy = (grp >> 4) * 2 + wide

    def along_z(to):
        return (base + to, wide)

    def along_xy(to):
        return ((to >> 1) * SIDE + zc, to & 1)

    mask_copy = pltpu.make_async_copy(mask, mask_ref, in_sem.at[2])
    occ_copy = pltpu.make_async_copy(occ, occb.at[0:NBF], in_sem.at[0])
    vir_copy = pltpu.make_async_copy(vir, virb, in_sem.at[1])
    pair_copy = pltpu.make_async_copy(pair, pair_ref, in_sem.at[3])

    def ao_copy(p):
        return pltpu.make_async_copy(ao.at[p], aob.at[p], ao_sem.at[p])

    for copy in (mask_copy, occ_copy, ao_copy(0), vir_copy, pair_copy):
        copy.start()

    barrier = pltpu.get_barrier_semaphore()
    for k in range(1, SIDE):
        for to in (along_z((zc + k) & (SIDE - 1)), along_xy((xy + k) & (SIDE - 1))):
            pl.semaphore_signal(barrier, inc=1, device_id=to, device_id_type=MESH)

    row = iota((NOCC, NOCC), 0)
    col = iota((NOCC, NOCC), 1)
    hi = lax.shift_right_logical(row, 4)
    lo = row & 15

    def owner(xy_of, zc_of):
        return (lax.shift_right_logical(xy_of, 1) * SIDE + zc_of) * 2 + (xy_of & 1)

    def spread_mask(p):
        block_of = iota((NBLK, NBP), 0) * BLK
        lane = iota((NBLK, NBP), 1)
        spread = one_hot((lane >= block_of) & (lane < block_of + BLK))
        mx[p, 0:NBLK] = dot(mask_ref[:, p, :].astype(F32).astype(BF16), spread, NN)

    scr[NBF:NBP, :] = jnp.zeros((NBP - NBF, NBP), BF16)
    scr[0:NBF, NBP - 128 : NBP] = jnp.zeros((NBF, 128), BF16)
    occb[NBF:NBP, :] = jnp.zeros((NBP - NBF, NOCC), BF16)
    virt[:, NBP - 128 : NBP] = jnp.zeros((NVP, 128), BF16)
    virt[WIDE:NVP, :] = jnp.zeros((NVP - WIDE, NBP), BF16)
    perm[0] = one_hot(col == owner(lo, hi))
    mask_copy.wait()
    spread_mask(0)
    occ_copy.wait()
    occt[0] = dot(perm[0], occb[...], NT).astype(BF16)

    def got(ref, sem):
        pltpu.make_async_copy(ref, ref, sem).wait()

    def slab(ref, k):
        return ref.at[pl.ds(pl.multiple_of(k * SIDE, SIDE), SIDE)]

    def spread_out(src, dst, me, to_device, sends, recvs, columns=slice(None)):
        for k in ORDER:
            to = (me + k) & (SIDE - 1)
            pltpu.make_async_remote_copy(
                src_ref=slab(src, to).at[:, columns], dst_ref=slab(dst, me).at[:, columns],
                send_sem=sends, recv_sem=recvs,
                device_id=to_device(to), device_id_type=MESH,
            ).start()
        slab(dst, me)[:, columns] = slab(src, me)[:, columns]

    def phase1(p, carry):
        q = p & 1
        ao_copy(p).wait()

        @pl.when(p < PAIRS_HERE - 1)
        def _():
            ao_copy(p + 1).start()


        def screen(r, c):
            rows = pl.ds(pl.multiple_of(r * BLK, BLK), BLK)
            keep = mx[p, pl.ds(r, 1), 0:NBF].astype(BF16)
            scr[rows, 0:NBF] = aob[p, rows, :] * keep
            return c

        lax.fori_loop(0, NBLK, screen, 0)
        left[...] = dot(occt[q], scr[...], NN).astype(BF16)

        @pl.when(p == 0)
        def _():
            vir_copy.wait()
            virt[0:NVIR, 0:NBF] = virb[...]

        half[p, :, 0:512] = dot(left[...], virt[0:512], NT).astype(BF16)

        @pl.when(p == 0)
        def _():
            pl.semaphore_wait(barrier, 2 * (SIDE - 1))

        @pl.when(q == 0)
        def _():
            spread_out(half.at[p], recv.at[p], zc, along_z, send1.at[p], recv1.at[p], slice(0, 512))

        both = dot(left[...], virt[512:NVP], NT)
        half[p, :, 512:WIDE] = both[:, 0 : WIDE - 512].astype(BF16)
        rest[p] = both[:, WIDE - 512 : NVP - 512].astype(BF16)

        @pl.when(q == 0)
        def _():
            spread_out(half.at[p], recv.at[p], zc, along_z, send1.at[p], recv1.at[p], slice(512, WIDE))

        @pl.when(q == 1)
        def _():
            spread_out(half.at[p], recv.at[p], xy, along_xy, send1.at[p], recv1.at[p])

        @pl.when(p == 0)
        def _():
            pair_copy.wait()
            lane_own = iota((1, 128), 1)
            own = jnp.zeros((1, 128), jnp.int32)
            for pair_here in range(PAIRS_HERE):
                for j in range(2):
                    value = pair_ref[j : j + 1, pair_here : pair_here + 1]
                    own = jnp.where(lane_own == 2 * pair_here + j, value, own)
            idx_own[...] = own
            idx_z[zc] = own
            for k in range(1, SIDE):
                pltpu.make_async_remote_copy(
                    src_ref=idx_own, dst_ref=idx_z.at[zc],
                    send_sem=idx_send.at[0], recv_sem=idx_recv.at[0],
                    device_id=along_z((zc + k) & (SIDE - 1)), device_id_type=MESH,
                ).start()
            perm[1] = one_hot(col == owner(hi, lo))
            perm[2] = one_hot(col == row)
            perm[3] = one_hot(col == lo * SIDE + hi)
            for pair_here in range(1, PAIRS_HERE):
                spread_mask(pair_here)
            occt[1] = dot(perm[1], occb[...], NT).astype(BF16)

        return carry

    lax.fori_loop(0, PAIRS_HERE, phase1, 0)

    lane_row = iota((128, 128), 0)
    lane_col = iota((128, 128), 1)
    total = jnp.zeros((NOCC, 128), F32)
    for p in range(PAIRS_HERE):
        moved = dot(rest[p], one_hot(((lane_col & 15) == lane_row + REST * p) & (lane_row < REST)), NN)
        if p % 2:
            moved = dot(perm[3], moved.astype(BF16), NN)
        total = total + moved
    rest_row = iota((NOCC, 128), 0)
    in_group = lax.shift_right_logical(iota((NOCC, 128), 1), 4) == (rest_row & 7)
    low_half = (rest_row & 8) == 0
    picked = jnp.where(in_group, total, 0.0).astype(BF16)
    fold_row = iota((SIDE, NOCC), 0)
    fold_col = iota((SIDE, NOCC), 1)
    for h in range(2):
        fold = (lax.shift_right_logical(fold_col, 4) == fold_row) & ((fold_col & 8) == 8 * h)
        rest_own[:, h, :] = dot(one_hot(fold), picked, NN)
    rest_z[zc] = rest_own[zc]
    for k in ORDER:
        to = (zc + k) & (SIDE - 1)
        pltpu.make_async_remote_copy(
            src_ref=rest_own.at[to], dst_ref=rest_z.at[zc],
            send_sem=rest_send.at[0], recv_sem=rest_sem.at[0],
            device_id=along_z(to), device_id_type=MESH,
        ).start()

    got(idx_z.at[0 : SIDE - 1], idx_recv.at[0])
    idx_zrow[...] = idx_z[:, 0, :]
    idx_all[xy] = idx_z[:, 0, :]

    for k in range(1, SIDE):
        pltpu.make_async_remote_copy(
            src_ref=idx_zrow, dst_ref=idx_all.at[xy],
            send_sem=idx_send.at[1], recv_sem=idx_recv.at[1],
            device_id=along_xy((xy + k) & (SIDE - 1)), device_id_type=MESH,
        ).start()

    lane_all = iota((NOCC, 128), 1)
    basis = iota((NOCC, NBP), 1)

    def build(p, c):
        table = idx_all[...].reshape(NOCC, 128).astype(F32)

        def chosen(j):
            return jnp.sum(jnp.where(lane_all == j, table, 0.0), axis=1, keepdims=True).astype(jnp.int32)

        lam = dot(one_hot(basis == chosen(2 * p)), occb[:, 0:128], NN)[:, 0:1]
        rows = dot(one_hot(basis == chosen(2 * p + 1)), virt[...], NT)
        kernel_rows = (lam * rows).astype(BF16)
        pk[p] = kernel_rows
        pkt[p] = dot(perm[2 + (p & 1)], kernel_rows, NN).astype(BF16)
        return c


    def phase2(p):
        got(recv.at[p, 0 : (SIDE - 1) * SIDE], recv1.at[p])
        turned[p] = dot(perm[3], recv[p], NN).astype(BF16)
        me, to_device = (zc, along_z) if p % 2 else (xy, along_xy)
        for part, columns in enumerate(parts_of(p)):
            spread_out(turned.at[p], final.at[p], me, to_device, send2.at[p], recv2.at[p, part], columns)

    def parts_of(p):
        return (slice(0, 512), slice(512, WIDE)) if p == PAIRS_HERE - 1 else (slice(0, WIDE),)

    def phase2_rest():
        got(rest_z.at[0 : SIDE - 1], rest_sem.at[0])
        source = one_hot(lax.shift_right_logical(iota((NOCC, SIDE), 0), 4) == iota((NOCC, SIDE), 1))
        halves = [dot(source, rest_z[:, h, :].astype(BF16), NN) for h in range(2)]
        unfolded = jnp.where(in_group, jnp.where(low_half, halves[0], halves[1]), 0.0).astype(BF16)
        unfold = one_hot(((lane_row & 15) == lane_col) & (lane_col < SIDE))
        received = dot(unfolded, unfold, NN).astype(BF16)
        rest_turned[...] = dot(perm[3], received, NN).astype(BF16)
        spread_out(rest_turned, rest_final, xy, along_xy, rest_send.at[1], rest_sem.at[1])

    def add_rest():
        got(rest_final.at[0 : (SIDE - 1) * SIDE], rest_sem.at[1])
        total = jnp.zeros((REST, NVP), F32)
        for p in range(PAIRS_HERE):
            total = total + dot(rest_final[...], pk[p], TN)[REST * p : REST * (p + 1)]
        out[WIDE:NVIR] = (total[:, 0:NVIR] * SCALE).astype(BF16)

    def add(p, first=False, last=False):
        for part, columns in enumerate(parts_of(p)):
            got(final.at[p, 0 : (SIDE - 1) * SIDE, columns], recv2.at[p, part])
            for a0 in range(columns.start, columns.stop, 256):
                rows = pl.ds(a0, min(256, WIDE - a0))
                term = dot(final[p, :, rows], pkt[p], TN)
                if not first:
                    term = acc[rows] + term
                if last:
                    out[rows] = (term[:, 0:NVIR] * SCALE).astype(BF16)
                else:
                    acc[rows] = term

    phase2(0)
    phase2(1)
    phase2(2)
    phase2(3)
    phase2_rest()
    got(idx_all.at[0 : SIDE - 1], idx_recv.at[1])
    lax.fori_loop(0, PAIRS_HERE, build, 0)
    add(0, first=True)
    add(2)
    add_rest()
    add(1)
    add(3, last=True)

    for p in range(PAIRS_HERE):
        got(half.at[p, 0 : (SIDE - 1) * SIDE], send1.at[p])
        got(turned.at[p, 0 : (SIDE - 1) * SIDE], send2.at[p])
    got(rest_own.at[0 : SIDE - 1], rest_send.at[0])
    got(rest_turned.at[0 : (SIDE - 1) * SIDE], rest_send.at[1])
    got(idx_z.at[0 : SIDE - 1], idx_send.at[0])
    got(idx_all.at[0 : SIDE - 1], idx_send.at[1])


def shards(ao_slab, screen_mask, pair_ao, occ_coef, vir_coef):
    hbm = pl.BlockSpec(memory_space=pltpu.HBM)
    arrays = (ao_slab, screen_mask.transpose(1, 0, 2), pair_ao.T, occ_coef, vir_coef.T)
    dma = pltpu.SemaphoreType.DMA
    block = pl.pallas_call(
        kernel,
        name="mo_block",
        out_shape=pltpu.VMEM((NVIR, NVIR), BF16),
        in_specs=[hbm] * 5,
        out_specs=pl.BlockSpec(memory_space=pltpu.VMEM),
        scratch_shapes=[
            pltpu.VMEM((NBLK, PAIRS_HERE, NBLK), jnp.int32),
            pltpu.VMEM((2, PAIRS_HERE), jnp.int32),
            pltpu.VMEM((PAIRS_HERE, NBF, NBF), BF16),
            pltpu.VMEM((NBP, NOCC), BF16),
            pltpu.VMEM((NVIR, NBF), BF16),
            pltpu.VMEM((NVP, NBP), BF16),
            pltpu.VMEM((2, NOCC, NBP), BF16),
            pltpu.VMEM((4, NOCC, NOCC), BF16),
            pltpu.VMEM((PAIRS_HERE, 32, NBP), F32),
            pltpu.VMEM((NBP, NBP), BF16),
            pltpu.VMEM((NOCC, NBP), BF16),
            pltpu.VMEM((PAIRS_HERE, NOCC, WIDE), BF16),
            pltpu.VMEM((PAIRS_HERE, NOCC, WIDE), BF16),
            pltpu.VMEM((PAIRS_HERE, NOCC, WIDE), BF16),
            pltpu.VMEM((PAIRS_HERE, NOCC, WIDE), BF16),
            pltpu.VMEM((PAIRS_HERE, NOCC, 128), BF16),
            pltpu.VMEM((SIDE, 2, 128), F32),
            pltpu.VMEM((SIDE, 2, 128), F32),
            pltpu.VMEM((NOCC, 128), BF16),
            pltpu.VMEM((NOCC, 128), BF16),
            pltpu.VMEM((PAIRS_HERE, NOCC, NVP), BF16),
            pltpu.VMEM((PAIRS_HERE, NOCC, NVP), BF16),
            pltpu.VMEM((WIDE, NVP), F32),
            pltpu.VMEM((1, 128), jnp.int32),
            pltpu.VMEM((SIDE, 1, 128), jnp.int32),
            pltpu.VMEM((SIDE, 128), jnp.int32),
            pltpu.VMEM((SIDE, SIDE, 128), jnp.int32),
            dma((PAIRS_HERE,)),
            dma((4,)),
            dma((PAIRS_HERE,)),
            dma((PAIRS_HERE,)),
            dma((PAIRS_HERE,)),
            dma((PAIRS_HERE, 2)),
            dma((2,)),
            dma((2,)),
            dma((2,)),
            dma((2,)),
        ],
        compiler_params=pltpu.CompilerParams(
            collective_id=0, has_side_effects=True, vmem_limit_bytes=56 << 20
        ),
        cost_estimate=pl.CostEstimate(flops=7_000_000_000, bytes_accessed=16_000_000, transcendentals=0),
    )(*(pltpu.with_memory_space_constraint(x, pltpu.HBM) for x in arrays))
    return block.reshape(1, NVIR, 1, NVIR)


def solution(mesh):
    in_specs = (
        P(("grp", "wide"), None, None),
        P(("grp", "wide"), None, None),
        P(("grp", "wide"), None),
        P(),
        P(),
    )
    out_specs = P(("grp", "wide"), None, None, None)
    return jax.shard_map(shards, mesh=mesh, in_specs=in_specs, out_specs=out_specs, check_vma=False)
```
